32 devices in a mesh: depth: 8 (over y, x, core), rows: 4 (over z).
Axes of the slice: x: 2, y: 2, z: 4, core: 2. Of those that a mesh axis runs over, the one named last changes fastest.
Arguments:
- initial: float32 [16, 256, 128], P('rows'), may hold values from -6 to 6
- forward_guess: float32 [16, 16, 256, 128], P('depth', 'rows'), may hold values from -6 to 6
- adjoint_guess: float32 [16, 16, 256, 128], P('depth', 'rows'), may hold values from -6 to 6
- cotangent: float32 [16, 256, 128], P('rows'), may hold values from -6 to 6
- kernel: bfloat16 [3, 3, 128, 128], replicated, may hold values from -0.125 to 0.125
- conv_bias: float32 [128], replicated, may hold values from -1.5 to 1.5
Outputs:
- states: float32 [16, 16, 256, 128], P('depth', 'rows')
- adjoints: float32 [16, 16, 256, 128], P('depth', 'rows')
- grad_kernel: float32 [3, 3, 128, 128], replicated
- grad_bias: float32 [128], replicated
The draws below stay inside these ranges and needn't reach their ends.
All inputs are finite; a program needn't handle non-finite values.
Results may differ from the reference program's by a relative error of at most 0.0025.
The reference program's roundings to bfloat16 on the way count: a program that leaves them out, or rounds other values in their place, can miss the bound.
Values may be sent and summed in bfloat16 or wider, within the bound.
A program may use at most 64 MiB of HBM per device.

```python
import jax
import jax.numpy as jnp
from jax import lax

C = 128
W = 256
H = 16
STEPS = 16


def level_of(key, dims, split, least, high):
    gain, own = 1.0, jax.random.fold_in(key, 6)
    for position, shards_of in split:
        steps = jnp.exp(jax.random.uniform(jax.random.fold_in(own, position), (shards_of,), jnp.float32, least / len(split), high / len(split)))
        gain = gain * jnp.repeat(steps, dims[position] // shards_of).reshape([-1 if axis == position else 1 for axis in range(len(dims))])
    return gain


def normal_values(key, shape, scale, reach, cuts=(), held_as=jnp.bfloat16):
    factor_of = level_of(key, shape, cuts, -0.22, 0.18) if cuts else 1.0
    drawn = jax.random.normal(key, shape, jnp.float32) * scale * factor_of
    return jnp.minimum(jnp.maximum(drawn, -reach), reach).astype(held_as)


def setup_inputs(seed: int = 0) -> dict:
    keys = jax.random.split(jax.random.key(seed), 7)
    return {
        "initial": normal_values(keys[0], (H, W, C), 1.0, 6.0, ((0, 4),), jnp.float32),
        "forward_guess": normal_values(keys[1], (STEPS, H, W, C), 1.0, 6.0, ((0, 8), (1, 4)), jnp.float32),
        "adjoint_guess": normal_values(keys[2], (STEPS, H, W, C), 1.0, 6.0, ((0, 8), (1, 4)), jnp.float32),
        "cotangent": normal_values(keys[3], (H, W, C), 1.0, 6.0, ((0, 4),), jnp.float32),
        "kernel": normal_values(keys[4], (3, 3, C, C), (18 * C) ** -0.5, 0.125),
        "conv_bias": normal_values(keys[5], (C,), 0.3, 1.5, (), jnp.float32),
    }


STEP_SIZE = 0.2


def restrict(signal):
    row_count, col_count, channels = signal.shape
    return signal.reshape(row_count // 2, 2, col_count // 2, 2, channels).mean(axis=(1, 3))


def prolong(signal):
    return jnp.repeat(jnp.repeat(signal, 2, axis=0), 2, axis=1)


def taps_product(padded, kernel, row_count, col_count):
    summed = jnp.zeros((row_count * col_count, kernel.shape[3]), jnp.float32)
    for row_tap in range(3):
        for col_tap in range(3):
            window = padded[row_tap:row_tap + row_count, col_tap:col_tap + col_count].reshape(row_count * col_count, -1)
            summed = summed + jnp.dot(window, kernel[row_tap, col_tap], preferred_element_type=jnp.float32)
    return summed.reshape(row_count, col_count, -1)


def surround(signal):
    return jnp.pad(signal, ((1, 1), (1, 1), (0, 0)))


def advance(current, kernel, conv_bias, on_coarse):
    factor = 2.0 * STEP_SIZE if on_coarse else STEP_SIZE
    squashed = jnp.tanh(current).astype(jnp.bfloat16)
    padded = surround(squashed)
    return current + factor * (taps_product(padded, kernel, current.shape[0], current.shape[1]) + conv_bias)


def retreat(current, adjoint, kernel_flip, on_coarse):
    factor = 2.0 * STEP_SIZE if on_coarse else STEP_SIZE
    derivative = 1.0 - jnp.tanh(current) ** 2
    padded = surround(adjoint.astype(jnp.bfloat16))
    return adjoint + factor * derivative * taps_product(padded, kernel_flip, adjoint.shape[0], adjoint.shape[1])


def kernel_terms(padded, cotan, row_count, col_count):
    flat = cotan.reshape(row_count * col_count, -1)
    tap_rows = []
    for row_tap in range(3):
        tap_cols = []
        for col_tap in range(3):
            window = padded[row_tap:row_tap + row_count, col_tap:col_tap + col_count].reshape(row_count * col_count, -1)
            tap_cols.append(lax.dot_general(window, flat, (((0,), (0,)), ((), ())), preferred_element_type=jnp.float32))
        tap_rows.append(jnp.stack(tap_cols))
    return jnp.stack(tap_rows)


def reference(initial, forward_guess, adjoint_guess, cotangent, kernel, conv_bias):
    n_steps = forward_guess.shape[0]
    half_count = n_steps // 2
    row_count, col_count = initial.shape[0], initial.shape[1]
    kernel_flip = jnp.transpose(jnp.flip(kernel, (0, 1)), (0, 1, 3, 2))
    guesses = [initial] + [forward_guess[n] for n in range(n_steps)]
    relaxed = [initial]
    for n in range(1, n_steps + 1):
        if n % 2 == 1:
            relaxed.append(advance(guesses[n - 1], kernel, conv_bias, False))
        else:
            relaxed.append(guesses[n])
    solution = restrict(initial)
    coarse_states = [solution]
    corrected = list(relaxed)
    for k in range(1, half_count + 1):
        rhs_here = restrict(advance(relaxed[2 * k - 1], kernel, conv_bias, False)) - advance(restrict(relaxed[2 * k - 2]), kernel, conv_bias, True)
        solution = advance(solution, kernel, conv_bias, True) + rhs_here
        coarse_states.append(solution)
        corrected[2 * k] = relaxed[2 * k] + prolong(solution - restrict(relaxed[2 * k]))
    fine_states = [initial]
    for n in range(1, n_steps + 1):
        if n % 2 == 1:
            fine_states.append(advance(corrected[n - 1], kernel, conv_bias, False))
        else:
            fine_states.append(corrected[n])
    targets = [adjoint_guess[n] for n in range(n_steps)] + [cotangent]
    primal = []
    for n in range(n_steps):
        if n % 2 == 1:
            primal.append(retreat(fine_states[n], targets[n + 1], kernel_flip, False))
        else:
            primal.append(targets[n])
    primal.append(cotangent)
    fixed = list(primal)
    correction = jnp.zeros_like(restrict(initial))
    for k in range(half_count - 1, -1, -1):
        residual = retreat(fine_states[2 * k], primal[2 * k + 1], kernel_flip, False) - primal[2 * k]
        correction = retreat(coarse_states[k], correction, kernel_flip, True) + restrict(residual)
        fixed[2 * k] = primal[2 * k] + prolong(correction)
    lambdas = []
    for n in range(n_steps):
        if n % 2 == 1:
            lambdas.append(retreat(fine_states[n], fixed[n + 1], kernel_flip, False))
        else:
            lambdas.append(fixed[n])
    lambdas.append(cotangent)
    grad_sum = jnp.zeros(kernel.shape, jnp.float32)
    bias_sum = jnp.zeros((kernel.shape[3],), jnp.float32)
    for n in range(n_steps):
        squashed = jnp.tanh(fine_states[n]).astype(jnp.bfloat16)
        grad_sum = grad_sum + kernel_terms(surround(squashed), lambdas[n + 1].astype(jnp.bfloat16), row_count, col_count)
        bias_sum = bias_sum + jnp.sum(lambdas[n + 1], axis=(0, 1))
    factor = STEP_SIZE / (row_count * col_count)
    states = jnp.stack(fine_states[1:])
    adjoints = jnp.stack(lambdas[:n_steps])
    return states, adjoints, grad_sum * factor, bias_sum * factor
```

```python
import functools

import jax
import jax.numpy as jnp
from jax import lax
from jax.experimental import pallas as pl
from jax.experimental.pallas import tpu as pltpu
from jax.sharding import PartitionSpec as P

STEP_SIZE = 0.2
MESH = pl.DeviceIdType.MESH
F32, BF16 = jnp.float32, jnp.bfloat16
SRC, ODD, PREV, AHEAD, RELAXED, FIXED = range(6)


def cycle(
    K, Z, cells, init_hbm, fg_hbm, ag_hbm, cot_hbm, kernel_ref, bias_ref,
    states_hbm, adjoints_hbm, gk_ref, gb_ref,
    g, src, init, gprev, y, ynext, cot,
    work, work2, colbuf, derive0, derive1, states, adjoints,
    sf, su, fh, fh_send, fh_recv,
    sc, ch, ch_send, ch_recv,
    vall, dall, eall, rhs, rhs_send, rhs_recv, res, res_send, res_recv, yc, yc_send, yc_recv,
    wf, wr, ga, go, rb, ar_send, ar_recv, big_send, big_recv, in_sem, out_sem,
):
    R, W, C = g.shape
    Rc, Wc = R // 2, W // 2
    d, z = lax.axis_index("depth"), lax.axis_index("rows")
    last = d == K - 1
    NR = ga.shape[0]

    loads = [
        (fg_hbm.at[1], g), (init_hbm, init), (ag_hbm.at[0], y), (cot_hbm, cot),
    ]
    loads = [pltpu.make_async_copy(a, b, in_sem.at[i]) for i, (a, b) in enumerate(loads)]

    def src_load(a):
        return pltpu.make_async_copy(a, src, in_sem.at[4])

    def prev_load():
        return pltpu.make_async_copy(init_hbm, gprev, in_sem.at[5])

    def next_load():
        return pltpu.make_async_copy(cot_hbm, ynext, in_sem.at[6])

    @pl.when(last)
    def _():
        src_load(init_hbm).start()
        next_load().start()

    @pl.when(d < K - 1)
    def _():
        src_load(fg_hbm.at[1]).start()

    for load in (loads[1], loads[0], loads[2], loads[3]):
        load.start()

    @pl.when(d == 0)
    def _():
        prev_load().start()

    barrier = pltpu.get_barrier_semaphore()
    for o in range(1, K):
        pl.semaphore_signal(barrier, inc=1, device_id=(lax.rem(d + o, K), z), device_id_type=MESH)
    for o in range(1, Z):
        pl.semaphore_signal(barrier, inc=1, device_id=(d, lax.rem(z + o, Z)), device_id_type=MESH)

    @pl.when(z == 0)
    def _():
        fh[:, 0] = jnp.zeros_like(fh[:, 0])
        ch[:, 0] = jnp.zeros_like(ch[:, 0])

    @pl.when(z == Z - 1)
    def _():
        fh[:, 1] = jnp.zeros_like(fh[:, 1])
        ch[:, 1] = jnp.zeros_like(ch[:, 1])

    for a in range(3):
        for b in range(3):
            wf[a * C : (a + 1) * C, b * C : (b + 1) * C] = kernel_ref[a, b]
            wr[a * C : (a + 1) * C, b * C : (b + 1) * C] = (
                kernel_ref[2 - a, 2 - b].astype(F32).T.astype(BF16)
            )
    bias = bias_ref[...]

    def remote(a, b, send, recv, target):
        return pltpu.make_async_remote_copy(
            src_ref=a, dst_ref=b, send_sem=send, recv_sem=recv, device_id=target, device_id_type=MESH
        )

    def halo_copies(buf, halo, send, recv, e):
        rows = buf.shape[1]
        up = remote(buf.at[e, 0], halo.at[e, 1], send.at[e, 0], recv.at[e, 1], (d, z - 1))
        down = remote(buf.at[e, rows - 1], halo.at[e, 0], send.at[e, 1], recv.at[e, 0], (d, z + 1))
        return up, down

    def from_up(buf, halo, send, recv, e):
        return remote(buf.at[e, 0], halo.at[e, 0], send.at[e, 1], recv.at[e, 0], (d, z - 1))

    def from_down(buf, halo, send, recv, e):
        return remote(buf.at[e, 0], halo.at[e, 1], send.at[e, 0], recv.at[e, 1], (d, z + 1))

    fine = (sf, fh, fh_send, fh_recv)
    coarse = (sc, ch, ch_send, ch_recv)

    def send_halo(group, e):
        up, down = halo_copies(*group, e)

        @pl.when(z > 0)
        def _():
            up.start()

        @pl.when(z < Z - 1)
        def _():
            down.start()

    def wait_halo(group, e):
        @pl.when(z > 0)
        def _():
            from_up(*group, e).wait_recv()

        @pl.when(z < Z - 1)
        def _():
            from_down(*group, e).wait_recv()

    def wait_sent(group, e):
        up, down = halo_copies(*group, e)

        @pl.when(z > 0)
        def _():
            up.wait_send()

        @pl.when(z < Z - 1)
        def _():
            down.wait_send()

    def col_sum(product, width):
        count = product.shape[0]
        col = lax.broadcasted_iota(jnp.int32, (count, C), 0) % width
        left = jnp.where(col == 0, 0.0, pltpu.roll(product[:, :C], 1, 0))
        right = jnp.where(col == width - 1, 0.0, pltpu.roll(product[:, 2 * C :], count - 1, 0))
        return product[:, C : 2 * C] + left + right

    def conv_own(s, weights):
        rows, width, _ = s.shape
        zero = jnp.zeros((1, width, C), BF16)
        above = jnp.concatenate([zero, s[:-1]], axis=0)
        below = jnp.concatenate([s[1:], zero], axis=0)
        lhs = jnp.concatenate([above, s, below], axis=2).reshape(rows * width, 3 * C)
        product = jnp.dot(lhs, weights[...], preferred_element_type=F32)
        return col_sum(product, width).reshape(rows, width, C)

    def conv_halo(halo, e, weights):
        up = jnp.dot(halo[e, 0], weights[:C], preferred_element_type=F32)
        down = jnp.dot(halo[e, 1], weights[2 * C :], preferred_element_type=F32)
        width = up.shape[0]
        return col_sum(up, width)[None], col_sum(down, width)[None]

    def add_edges(own, up, down):
        inner = [own[1:-1]] if own.shape[0] > 2 else []
        return jnp.concatenate([own[:1] + up] + inner + [own[-1:] + down], axis=0)

    def conv(group, e, weights):
        own = conv_own(group[0][e], weights)
        wait_halo(group, e)
        return add_edges(own, *conv_halo(group[1], e, weights))

    def restrict(ref):
        def part(i, o):
            return ref[i, pl.ds(o, Wc, stride=2), :]

        rows = [
            (part(2 * i, 0) + part(2 * i, 1) + part(2 * i + 1, 0) + part(2 * i + 1, 1)) * 0.25
            for i in range(Rc)
        ]
        return jnp.stack(rows)

    def prolong(value):
        for i in range(Rc):
            colbuf[i, pl.ds(0, Wc, stride=2), :] = value[i]
            colbuf[i, pl.ds(1, Wc, stride=2), :] = value[i]
        wide = colbuf[...]
        return jnp.broadcast_to(wide[:, None], (Rc, 2, W, C)).reshape(R, W, C)

    def spread(buf, send, recv, slot):
        for o in range(1, K):
            remote(buf.at[slot], buf.at[slot], send.at[o], recv.at[slot], (lax.rem(d + o, K), z)).start()

    def wait_panel(buf, send, recv, slot):
        remote(buf.at[slot], buf.at[slot], send.at[0], recv.at[slot], (lax.rem(d + 1, K), z)).wait_recv()

    def wait_spread(buf, send, recv, slot):
        for o in range(1, K):
            remote(
                buf.at[slot], buf.at[slot], send.at[o], recv.at[slot], (lax.rem(d + o, K), z)
            ).wait_send()

    src_load(init_hbm).wait()
    s = jnp.tanh(src[...]).astype(BF16)
    sf[SRC] = s
    src_c = restrict(src)
    sc[K] = jnp.tanh(src_c).astype(BF16)
    pl.semaphore_wait(barrier, K + Z - 2)
    send_halo(fine, SRC)
    send_halo(coarse, K)
    loads[1].wait()
    vall[0] = restrict(init)

    work[...] = src[...] + STEP_SIZE * (conv(fine, SRC, wf) + bias)
    sf[ODD] = jnp.tanh(work[...]).astype(BF16)
    send_halo(fine, ODD)
    tau = src_c + 2.0 * STEP_SIZE * (conv(coarse, K, wf) + bias)
    work[...] = work[...] + STEP_SIZE * (conv(fine, ODD, wf) + bias)
    own_panel = lax.rem(d + 1, K)
    rhs[own_panel] = (restrict(work) - tau).astype(BF16)
    spread(rhs, rhs_send, rhs_recv, own_panel)

    for load in (loads[0], loads[2], loads[3]):
        load.wait()
    to_next = remote(g, gprev, big_send.at[0], big_recv.at[0], (d + 1, z))
    to_prev = remote(y, ynext, big_send.at[1], big_recv.at[1], (d - 1, z))

    @pl.when(d < K - 1)
    def _():
        to_next.start()

    @pl.when(d > 0)
    def _():
        to_prev.start()

    yc[d] = restrict(y)
    yc[K] = restrict(cot)
    spread(yc, yc_send, yc_recv, d)

    def forward(k, carry):
        current = vall[k]
        t = jnp.tanh(current)
        sc[k] = t.astype(BF16)
        send_halo(coarse, k)
        dall[k] = 1.0 - t * t
        summed = conv(coarse, k, wf)

        @pl.when(k != own_panel)
        def _():
            wait_panel(rhs, rhs_send, rhs_recv, k)

        vall[k + 1] = current + 2.0 * STEP_SIZE * (summed + bias) + rhs[k].astype(F32)
        return carry

    lax.fori_loop(0, K, forward, 0)

    @pl.when(d > 0)
    def _():
        remote(g, gprev, big_send.at[0], big_recv.at[0], (d - 1, z)).wait_recv()

    @pl.when(d == 0)
    def _():
        prev_load().wait()

    work[...] = gprev[...] + prolong(vall[d] - restrict(gprev))
    t = jnp.tanh(work[...])
    sf[PREV] = t.astype(BF16)
    send_halo(fine, PREV)
    derive0[...] = 1.0 - t * t

    @pl.when(d < K - 1)
    def _():
        remote(y, ynext, big_send.at[1], big_recv.at[1], (d + 1, z)).wait_recv()

    @pl.when(last)
    def _():
        next_load().wait()

    sf[AHEAD] = ynext[...].astype(BF16)
    send_halo(fine, AHEAD)
    states[0] = work[...] + STEP_SIZE * (conv(fine, PREV, wf) + bias)
    t = jnp.tanh(states[0])
    su[...] = t.astype(BF16)
    derive1[...] = 1.0 - t * t
    work[...] = derive1[...] * conv(fine, AHEAD, wr)
    sf[RELAXED] = (ynext[...] + STEP_SIZE * work[...]).astype(BF16)
    send_halo(fine, RELAXED)
    states[1] = g[...] + prolong(vall[d + 1] - restrict(g))
    states_out = pltpu.make_async_copy(states, states_hbm, out_sem.at[0])
    states_out.start()
    work2[...] = work[...] + derive0[...] * conv(fine, RELAXED, wr)
    res[d] = (STEP_SIZE * restrict(work2)).astype(BF16)
    spread(res, res_send, res_recv, d)

    def panel(k):
        @pl.when(k != d)
        def _():
            wait_panel(res, res_send, res_recv, k)
            wait_panel(yc, yc_send, yc_recv, k)

        return res[k].astype(F32) + (yc[k + 1] - yc[k])

    eall[K] = jnp.zeros_like(eall[K])
    eall[K - 1] = panel(K - 1)

    def backward(i, carry):
        k = K - 2 - i
        error = eall[k + 1]
        slot = K + 1 + i
        sc[slot] = error.astype(BF16)
        send_halo(coarse, slot)
        summed = conv(coarse, slot, wr)
        eall[k] = error + 2.0 * STEP_SIZE * dall[k] * summed + panel(k)
        return carry

    lax.fori_loop(0, K - 1, backward, 0)

    work[...] = ynext[...] + prolong(eall[d + 1])
    sf[FIXED] = work[...].astype(BF16)
    send_halo(fine, FIXED)
    adjoints[0] = y[...] + prolong(eall[d])
    adjoints[1] = work[...] + STEP_SIZE * derive1[...] * conv(fine, FIXED, wr)
    adjoints_out = pltpu.make_async_copy(adjoints, adjoints_hbm, out_sem.at[1])
    adjoints_out.start()

    def col_taps(value):
        rows, width, _ = value.shape
        count = rows * width
        flat = value.astype(F32).reshape(count, C)
        col = lax.broadcasted_iota(jnp.int32, (count, C), 0) % width
        first = jnp.where(col == width - 1, 0.0, pltpu.roll(flat, count - 1, 0))
        third = jnp.where(col == 0, 0.0, pltpu.roll(flat, 1, 0))
        taps = jnp.concatenate([first.astype(BF16), flat.astype(BF16), third.astype(BF16)], axis=1)
        return taps.reshape(rows, width, 3 * C)

    def over_cells(a, b):
        return lax.dot_general(
            a.reshape(R * W, -1), b.reshape(R * W, -1), (((0,), (0,)), ((), ())), preferred_element_type=F32
        )

    taps = col_taps(jnp.concatenate([fh[FIXED, 0][None], sf[FIXED], fh[FIXED, 1][None]], axis=0))
    own = su[...]
    odd = [over_cells(own, taps[2 - a : 2 - a + R]) for a in range(3)]
    around = jnp.concatenate([fh[PREV, 0][None], sf[PREV], fh[PREV, 1][None]], axis=0)
    taps = col_taps(adjoints[1].astype(BF16))
    for a in range(3):
        even = over_cells(around[a : a + R], taps)
        for b in range(3):
            at = (3 * a + b) * C
            cols = slice(b * C, (b + 1) * C)
            ga[at : at + C] = even[:, cols] + odd[a][:, cols]
    total = jnp.sum((adjoints[1] + work[...]).reshape(R * W, C), axis=0, keepdims=True)
    ga[9 * C :] = jnp.zeros((NR - 9 * C, C), F32)
    ga[9 * C : 9 * C + 8] = jnp.broadcast_to(total, (8, C))

    core = lax.rem(d, 2)

    def split(index, stride):
        bit = lax.rem(index // stride, 2)
        return bit, index + (1 - 2 * bit) * stride

    depth_bits = [1 << i for i in range(K.bit_length() - 1)]
    swapped = depth_bits[:1] + depth_bits[1:][::-1]
    plan = []
    for one, two in zip(depth_bits, swapped):
        bit1, to1 = split(d, one)
        bit2, to2 = split(d, two)
        plan.append((bit1 * (1 - core) + bit2 * core, (to1 * (1 - core) + to2 * core, z)))
    for stride in [1 << i for i in range(Z.bit_length() - 1)]:
        bit, to = split(z, stride)
        plan.append((bit, (d, to)))
    n = len(plan)
    offset, length, place = 0, NR, 0
    sends, trail = [], []
    for i, (bit, to) in enumerate(plan):
        half = length // 2
        away = pl.multiple_of(offset + (1 - bit) * half, 8)
        offset = pl.multiple_of(offset + bit * half, 8)
        move = remote(
            ga.at[pl.ds(away, half)], rb.at[pl.ds(place, half)], ar_send.at[i], ar_recv.at[i], to
        )
        move.start()
        move.wait_recv()
        sends.append(move)
        ga[pl.ds(offset, half)] += rb[pl.ds(place, half)]
        trail.append((offset, half, to, away))
        place += half
        length = half
    go[pl.ds(offset, length)] = ga[pl.ds(offset, length)] * (STEP_SIZE / cells)
    for i, (offset, half, to, away) in reversed(list(enumerate(trail))):
        mine, other = go.at[pl.ds(offset, half)], go.at[pl.ds(away, half)]
        move = remote(mine, mine, ar_send.at[n + i], ar_recv.at[n + i], to)
        move.start()
        remote(mine, other, ar_send.at[n + i], ar_recv.at[n + i], to).wait_recv()
        sends.append(move)
    gk_ref[...] = go[: 9 * C]
    gb_ref[...] = go[9 * C : 9 * C + 8]

    for move in sends:
        move.wait_send()
    for e in range(6):
        wait_sent(fine, e)

    def sent(e, carry):
        wait_sent(coarse, e)
        return carry

    lax.fori_loop(0, 2 * K, sent, 0)
    wait_spread(rhs, rhs_send, rhs_recv, own_panel)
    wait_spread(res, res_send, res_recv, d)
    wait_spread(yc, yc_send, yc_recv, d)

    @pl.when(d < K - 1)
    def _():
        to_next.wait_send()

    @pl.when(d > 0)
    def _():
        to_prev.wait_send()

    states_out.wait()
    adjoints_out.wait()


def shards(K, Z, initial, forward_guess, adjoint_guess, cotangent, kernel, conv_bias):
    R, W, C = initial.shape
    Rc, Wc = R // 2, W // 2
    unit = 8 * K * Z
    NR = -(-(9 * C + 8) // unit) * unit
    bits = (K.bit_length() - 1) + (Z.bit_length() - 1)
    vmem, dma = pltpu.VMEM, pltpu.SemaphoreType.DMA
    field, coarse = vmem((R, W, C), F32), (Rc, Wc, C)
    scratch = (
        [field] * 7
        + [field, field, vmem((Rc, W, C), F32), field, field]
        + [vmem((2, R, W, C), F32)] * 2
        + [vmem((6, R, W, C), BF16), vmem((R, W, C), BF16), vmem((6, 2, W, C), BF16)]
        + [dma((6, 2)), dma((6, 2))]
        + [vmem((2 * K,) + coarse, BF16), vmem((2 * K, 2, Wc, C), BF16)]
        + [dma((2 * K, 2)), dma((2 * K, 2))]
        + [vmem((K + 1,) + coarse, F32), vmem((K,) + coarse, F32), vmem((K + 1,) + coarse, F32)]
        + [vmem((K,) + coarse, BF16), dma((K,)), dma((K,))] * 2
        + [vmem((K + 1,) + coarse, F32), dma((K,)), dma((K,))]
        + [vmem((3 * C, 3 * C), BF16)] * 2
        + [vmem((NR, C), F32)] * 3
        + [dma((2 * bits,)), dma((2 * bits,)), dma((2,)), dma((2,)), dma((7,)), dma((2,))]
    )
    any_spec, vmem_spec = pl.BlockSpec(memory_space=pl.ANY), pl.BlockSpec(memory_space=pltpu.VMEM)
    flops = 2 * 9 * C * C * R * W * 12
    states, adjoints, grad, bias = pl.pallas_call(
        functools.partial(cycle, K, Z, R * Z * W),
        out_shape=(
            jax.ShapeDtypeStruct((2, R, W, C), F32),
            jax.ShapeDtypeStruct((2, R, W, C), F32),
            jax.ShapeDtypeStruct((9 * C, C), F32),
            jax.ShapeDtypeStruct((8, C), F32),
        ),
        in_specs=[any_spec] * 4 + [vmem_spec] * 2,
        out_specs=(any_spec, any_spec, vmem_spec, vmem_spec),
        scratch_shapes=scratch,
        compiler_params=pltpu.CompilerParams(
            collective_id=0, has_side_effects=True, vmem_limit_bytes=56 * 1024 * 1024
        ),
        cost_estimate=pl.CostEstimate(flops=flops, bytes_accessed=24 * R * W * C, transcendentals=8 * R * W * C),
    )(initial, forward_guess, adjoint_guess, cotangent, kernel, conv_bias[None])
    return states, adjoints, grad.reshape(3, 3, C, C), bias[0]


def solution(mesh):
    placed = (
        P("rows", None, None),
        P("depth", "rows", None, None),
        P("depth", "rows", None, None),
        P("rows", None, None),
        P(),
        P(),
    )
    return jax.shard_map(
        functools.partial(shards, mesh.shape["depth"], mesh.shape["rows"]),
        mesh=mesh,
        in_specs=placed,
        out_specs=(P("depth", "rows", None, None), P("depth", "rows", None, None), P(), P()),
        check_vma=False,
    )
```

```python
import functools

import jax
import jax.numpy as jnp
from jax import lax
from jax.experimental import pallas as pl
from jax.experimental.pallas import tpu as pltpu
from jax.sharding import PartitionSpec as P

STEP_SIZE = 0.2
MESH = pl.DeviceIdType.MESH
F32, BF16 = jnp.float32, jnp.bfloat16
SRC, ODD, PREV, AHEAD, RELAXED, FIXED = range(6)


def cycle(
    K, Z, cells, init_hbm, fg_hbm, ag_hbm, cot_hbm, kernel_ref, bias_ref,
    states_hbm, adjoints_hbm, gk_ref,
    g, src, init, gprev, y, ynext, cot,
    work, work2, colbuf, derive0, derive1, states, adjoints,
    sf, su, fh, fh_send, fh_recv,
    st, th, th_send, th_recv,
    sc, ch, ch_send, ch_recv,
    vall, dall, fall, rprev, rnext, rown,
    rhs_all, rhs, rhs_send, rhs_recv, res_all, res, res_send, res_recv, yc_all, yc, yc_send, yc_recv,
    vx, vx_send, vx_recv, fx, fx_send, fx_recv,
    wf, wr, prev_t, odd_t, ga, rb1, rb2, rb3, gob, ar_send, ar_recv, big_send, big_recv, in_sem, out_sem,
):
    R, W, C = g.shape
    Rc, Wc = R // 2, W // 2
    Rh = Rc // 2
    d, z = lax.axis_index("depth"), lax.axis_index("rows")
    last = d == K - 1
    NR = ga.shape[0]
    core = lax.rem(d, 2)
    peer = d + 1 - 2 * core
    pair = d - core
    mine = pl.ds(core * Rh, Rh)

    loads = [
        (fg_hbm.at[1], g), (init_hbm, init), (ag_hbm.at[0], y), (cot_hbm, cot),
    ]
    loads = [pltpu.make_async_copy(a, b, in_sem.at[i]) for i, (a, b) in enumerate(loads)]

    def src_load(a):
        return pltpu.make_async_copy(a, src, in_sem.at[4])

    def prev_load():
        return pltpu.make_async_copy(init_hbm, gprev, in_sem.at[5])

    def next_load():
        return pltpu.make_async_copy(cot_hbm, ynext, in_sem.at[6])

    @pl.when(last)
    def _():
        src_load(init_hbm).start()
        next_load().start()

    @pl.when(d < K - 1)
    def _():
        src_load(fg_hbm.at[1]).start()

    for load in loads:
        load.start()

    @pl.when(d == 0)
    def _():
        prev_load().start()

    has_up, has_down = core + z > 0, z + core < Z
    up_target, down_target = (peer, z - 1 + core), (peer, z + core)

    barrier = pltpu.get_barrier_semaphore()
    for o in range(1, K):
        pl.semaphore_signal(barrier, inc=1, device_id=(lax.rem(d + o, K), z), device_id_type=MESH)
    for o in range(1, Z):
        pl.semaphore_signal(barrier, inc=1, device_id=(d, lax.rem(z + o, Z)), device_id_type=MESH)
    across = z + 2 * core - 1
    has_across = (across >= 0) & (across < Z)

    @pl.when(has_across)
    def _():
        pl.semaphore_signal(barrier, inc=1, device_id=(peer, across), device_id_type=MESH)

    @pl.when(z == 0)
    def _():
        fh[:, 0] = jnp.zeros_like(fh[:, 0])
        th[:, 0] = jnp.zeros_like(th[:, 0])

    @pl.when(z == Z - 1)
    def _():
        fh[:, 1] = jnp.zeros_like(fh[:, 1])
        th[:, 1] = jnp.zeros_like(th[:, 1])

    @pl.when(core + z == 0)
    def _():
        ch[:, 0] = jnp.zeros_like(ch[:, 0])

    @pl.when(z + core == Z)
    def _():
        ch[:, 1] = jnp.zeros_like(ch[:, 1])

    for a in range(3):
        for b in range(3):
            wf[a * C : (a + 1) * C, b * C : (b + 1) * C] = kernel_ref[a, b]
    bias = bias_ref[...]

    def remote(a, b, send, recv, target):
        return pltpu.make_async_remote_copy(
            src_ref=a, dst_ref=b, send_sem=send, recv_sem=recv, device_id=target, device_id_type=MESH
        )

    rows_line = (z > 0, z < Z - 1, (d, z - 1), (d, z + 1))
    fine = (sf, fh, fh_send, fh_recv) + rows_line
    tau_group = (st, th, th_send, th_recv) + rows_line
    coarse = (sc, ch, ch_send, ch_recv, has_up, has_down, up_target, down_target)

    def halo_copies(group, e):
        buf, halo, send, recv, _, _, above, below = group
        rows = buf.shape[1]
        up = remote(buf.at[e, 0], halo.at[e, 1], send.at[e, 0], recv.at[e, 1], above)
        down = remote(buf.at[e, rows - 1], halo.at[e, 0], send.at[e, 1], recv.at[e, 0], below)
        return up, down

    def send_halo(group, e):
        up, down = halo_copies(group, e)

        @pl.when(group[4])
        def _():
            up.start()

        @pl.when(group[5])
        def _():
            down.start()

    def wait_halo(group, e):
        buf, halo, send, recv, from_up, from_down, above, below = group

        @pl.when(from_up)
        def _():
            remote(buf.at[e, 0], halo.at[e, 0], send.at[e, 1], recv.at[e, 0], above).wait_recv()

        @pl.when(from_down)
        def _():
            remote(buf.at[e, 0], halo.at[e, 1], send.at[e, 0], recv.at[e, 1], below).wait_recv()

    def wait_sent(group, e):
        up, down = halo_copies(group, e)

        @pl.when(group[4])
        def _():
            up.wait_send()

        @pl.when(group[5])
        def _():
            down.wait_send()

    def col_sum(product, width):
        count = product.shape[0]
        col = lax.broadcasted_iota(jnp.int32, (count, C), 0) % width
        left = jnp.where(col == 0, 0.0, pltpu.roll(product[:, :C], 1, 0))
        right = jnp.where(col == width - 1, 0.0, pltpu.roll(product[:, 2 * C :], count - 1, 0))
        return product[:, C : 2 * C] + left + right

    def conv_own(s, weights):
        rows, width, _ = s.shape
        zero = jnp.zeros((1, width, C), BF16)
        above = jnp.concatenate([zero, s[:-1]], axis=0)
        below = jnp.concatenate([s[1:], zero], axis=0)
        lhs = jnp.concatenate([above, s, below], axis=2).reshape(rows * width, 3 * C)
        product = jnp.dot(lhs, weights[...], preferred_element_type=F32)
        return col_sum(product, width).reshape(rows, width, C)

    def conv_halo(halo, e, weights):
        up = jnp.dot(halo[e, 0], weights[:C], preferred_element_type=F32)
        down = jnp.dot(halo[e, 1], weights[2 * C :], preferred_element_type=F32)
        width = up.shape[0]
        return col_sum(up, width)[None], col_sum(down, width)[None]

    def add_edges(own, up, down):
        if own.shape[0] == 1:
            return own + up + down
        inner = [own[1:-1]] if own.shape[0] > 2 else []
        return jnp.concatenate([own[:1] + up] + inner + [own[-1:] + down], axis=0)

    def conv(group, e, weights, fill=None):
        buf, halo = group[:2]
        if buf.shape[1] == 1:
            own = jnp.dot(buf[e, 0], weights[C : 2 * C], preferred_element_type=F32)
            if fill is not None:
                fill()
            wait_halo(group, e)
            sides = jnp.concatenate([halo[e, 0], halo[e, 1]], axis=1)
            outer = jnp.concatenate([weights[:C], weights[2 * C :]], axis=0)
            product = own + jnp.dot(sides, outer, preferred_element_type=F32)
            return col_sum(product, product.shape[0])[None]
        own = conv_own(buf[e], weights)
        if fill is not None:
            fill()
        wait_halo(group, e)
        return add_edges(own, *conv_halo(halo, e, weights))

    def restrict(ref):
        def part(i, o):
            return ref[i, pl.ds(o, Wc, stride=2), :]

        rows = [
            (part(2 * i, 0) + part(2 * i, 1) + part(2 * i + 1, 0) + part(2 * i + 1, 1)) * 0.25
            for i in range(Rc)
        ]
        return jnp.stack(rows)

    def prolong(value):
        for i in range(Rc):
            colbuf[i, pl.ds(0, Wc, stride=2), :] = value[i]
            colbuf[i, pl.ds(1, Wc, stride=2), :] = value[i]
        wide = colbuf[...]
        return jnp.broadcast_to(wide[:, None], (Rc, 2, W, C)).reshape(R, W, C)

    def panel_copies(full, buf, send, recv, slot):
        copies = []
        for o in range(1, K):
            to = lax.rem(d + o, K)
            part = full.at[pl.ds(lax.rem(to, 2) * Rh, Rh)]
            copies.append(remote(part, buf.at[slot], send.at[o], recv.at[slot], (to, z)))
        return copies

    def spread(full, buf, send, recv, slot):
        for copy in panel_copies(full, buf, send, recv, slot):
            copy.start()
        buf[slot] = full[mine]

    def wait_spread(full, buf, send, recv, slot):
        for copy in panel_copies(full, buf, send, recv, slot):
            copy.wait_send()

    def wait_panel(buf, send, recv, slot):
        remote(buf.at[slot], buf.at[slot], send.at[0], recv.at[slot], (peer, z)).wait_recv()

    def share_copy(buf, send, recv, j):
        part = buf.at[j, mine]
        return remote(part, part, send.at[j], recv.at[j], (peer, z))

    def share(buf, send, recv, k, value):
        @pl.when((k >= pair) & (k <= pair + 2))
        def _():
            buf[k - pair, mine] = value
            share_copy(buf, send, recv, k - pair).start()

    def wait_shared(buf, send, recv):
        for j in range(3):
            share_copy(buf, send, recv, j).wait_recv()

    @pl.when(last)
    def _():
        src_load(init_hbm).wait()

    @pl.when(d < K - 1)
    def _():
        src_load(fg_hbm.at[1]).wait()

    sf[SRC] = jnp.tanh(src[...]).astype(BF16)
    pl.semaphore_wait(barrier, K + Z - 2 + has_across.astype(jnp.int32))

    send_halo(fine, SRC)
    src_c = restrict(src)
    st[0] = jnp.tanh(src_c).astype(BF16)
    send_halo(tau_group, 0)

    loads[0].wait()
    loads[2].wait()
    to_next = remote(g, gprev, big_send.at[0], big_recv.at[0], (d + 1, z))
    to_prev = remote(y, ynext, big_send.at[1], big_recv.at[1], (d - 1, z))

    @pl.when(d < K - 1)
    def _():
        to_next.start()

    @pl.when(d > 0)
    def _():
        to_prev.start()

    work[...] = src[...] + STEP_SIZE * (conv(fine, SRC, wf) + bias)
    sf[ODD] = jnp.tanh(work[...]).astype(BF16)
    send_halo(fine, ODD)
    tau = src_c + 2.0 * STEP_SIZE * (conv(tau_group, 0, wf) + bias)
    work[...] = work[...] + STEP_SIZE * (conv(fine, ODD, wf) + bias)
    own_panel = lax.rem(d + 1, K)
    rhs_all[...] = (restrict(work) - tau).astype(BF16)
    spread(rhs_all, rhs, rhs_send, rhs_recv, own_panel)

    loads[1].wait()
    colbuf[:, :Wc] = restrict(init)
    vall[0] = colbuf[mine, :Wc]
    share(vx, vx_send, vx_recv, 0, vall[0])
    loads[3].wait()
    rown[...] = restrict(y)
    yc_all[...] = rown[...].astype(BF16)
    spread(yc_all, yc, yc_send, yc_recv, d)
    for a in range(3):
        for b in range(3):
            wr[a * C : (a + 1) * C, b * C : (b + 1) * C] = (
                kernel_ref[2 - a, 2 - b].astype(F32).T.astype(BF16)
            )

    def ahead_arrives():
        @pl.when(d < K - 1)
        def _():
            remote(y, ynext, big_send.at[1], big_recv.at[1], (d + 1, z)).wait_recv()

        @pl.when(last)
        def _():
            next_load().wait()

        sf[AHEAD] = ynext[...].astype(BF16)
        send_halo(fine, AHEAD)

    def ahead_conv():
        work2[...] = conv(fine, AHEAD, wr)

    def prev_arrives():
        @pl.when(d > 0)
        def _():
            remote(g, gprev, big_send.at[0], big_recv.at[0], (d - 1, z)).wait_recv()

        @pl.when(d == 0)
        def _():
            prev_load().wait()

        rprev[...] = restrict(gprev)

    def next_restricted():
        rnext[...] = restrict(ynext)

    def filled(k, steps, tasks):
        for i, task in enumerate(tasks):
            pl.when(k == max(0, steps - len(tasks) + i))(task)

    def forward(k, current):
        t = jnp.tanh(current)
        sc[k] = t.astype(BF16)
        send_halo(coarse, k)
        dall[k] = 1.0 - t * t

        def fill():
            filled(k, K, [ahead_arrives, next_restricted, ahead_conv, prev_arrives])

        summed = conv(coarse, k, wf, fill)

        @pl.when(k != own_panel)
        def _():
            wait_panel(rhs, rhs_send, rhs_recv, k)

        value = current + 2.0 * STEP_SIZE * (summed + bias) + rhs[k].astype(F32)
        share(vx, vx_send, vx_recv, k + 1, value)
        return value

    lax.fori_loop(0, K, forward, vall[0])
    wait_shared(vx, vx_send, vx_recv)

    work[...] = gprev[...] + prolong(vx[core] - rprev[...])
    t = jnp.tanh(work[...])
    sf[PREV] = t.astype(BF16)
    send_halo(fine, PREV)
    derive0[...] = 1.0 - t * t
    states[0] = work[...] + STEP_SIZE * (conv(fine, PREV, wf) + bias)
    t = jnp.tanh(states[0])
    su[...] = t.astype(BF16)
    slope = 1.0 - t * t
    derive1[...] = slope
    work[...] = slope * work2[...]
    sf[RELAXED] = (ynext[...] + STEP_SIZE * work[...]).astype(BF16)
    send_halo(fine, RELAXED)
    work2[...] = work[...] + derive0[...] * conv(fine, RELAXED, wr)
    res_all[...] = (STEP_SIZE * restrict(work2)).astype(BF16)
    spread(res_all, res, res_send, res_recv, d)
    colbuf[:, :Wc] = restrict(cot)
    fall[K] = colbuf[mine, :Wc]
    share(fx, fx_send, fx_recv, K, fall[K])

    def panel(k):
        @pl.when(k != d)
        def _():
            wait_panel(res, res_send, res_recv, k)
            wait_panel(yc, yc_send, yc_recv, k)

        return res[k].astype(F32)

    states_out = pltpu.make_async_copy(states, states_hbm, out_sem.at[0])

    def corrected_state():
        states[1] = g[...] + prolong(vx[core + 1] - restrict(g))
        states_out.start()

    def turn(rows, out):
        for i, row in enumerate(rows):
            out[:, i * W : (i + 1) * W] = row.astype(F32).T.astype(BF16)

    def turn_prev():
        turn([fh[PREV, 0]] + [sf[PREV, i] for i in range(R)] + [fh[PREV, 1]], prev_t)

    def turn_odd():
        turn([su[i] for i in range(R)], odd_t)

    value = fall[K] + panel(K - 1)
    share(fx, fx_send, fx_recv, K - 1, value)

    def backward(i, later):
        k = K - 2 - i
        sc[K + i] = (later - yc[k + 1].astype(F32)).astype(BF16)
        send_halo(coarse, K + i)

        def fill():
            filled(i, K - 1, [corrected_state, turn_prev, turn_odd])

        summed = conv(coarse, K + i, wr, fill)
        value = later + 2.0 * STEP_SIZE * dall[k] * summed + panel(k)
        share(fx, fx_send, fx_recv, k, value)
        return value

    lax.fori_loop(0, K - 1, backward, value)
    wait_shared(fx, fx_send, fx_recv)

    work[...] = ynext[...] + prolong(fx[core + 1] - rnext[...])
    sf[FIXED] = work[...].astype(BF16)
    send_halo(fine, FIXED)
    adjoints[0] = y[...] + prolong(fx[core] - rown[...])
    adjoints[1] = work[...] + STEP_SIZE * derive1[...] * conv(fine, FIXED, wr)
    adjoints_out = pltpu.make_async_copy(adjoints, adjoints_hbm, out_sem.at[1])
    adjoints_out.start()

    def col_taps(value):
        rows, width, _ = value.shape
        count = rows * width
        flat = value.astype(F32).reshape(count, C)
        col = lax.broadcasted_iota(jnp.int32, (count, C), 0) % width
        first = jnp.where(col == width - 1, 0.0, pltpu.roll(flat, count - 1, 0))
        third = jnp.where(col == 0, 0.0, pltpu.roll(flat, 1, 0))
        taps = jnp.concatenate([first.astype(BF16), flat.astype(BF16), third.astype(BF16)], axis=1)
        return taps.reshape(rows, width, 3 * C)

    taps = col_taps(jnp.concatenate([fh[FIXED, 0][None], sf[FIXED], fh[FIXED, 1][None]], axis=0))
    taps = jnp.concatenate([taps[2 - a : 2 - a + R] for a in range(3)], axis=2).reshape(R * W, 9 * C)
    odd = jnp.dot(odd_t[...], taps, preferred_element_type=F32)
    taps = col_taps(adjoints[1].astype(BF16)).reshape(R * W, 3 * C)
    for a in range(3):
        even = jnp.dot(prev_t[:, a * W : (a + R) * W], taps, preferred_element_type=F32)
        for b in range(3):
            at = (3 * a + b) * C
            ga[at : at + C] = even[:, b * C : (b + 1) * C] + odd[:, at : at + C]
    total = jnp.sum((adjoints[1] + work[...]).reshape(R * W, C), axis=0, keepdims=True)
    ga[9 * C :] = jnp.zeros((NR - 9 * C, C), F32)
    ga[9 * C : 9 * C + 8] = jnp.broadcast_to(total, (8, C))

    chips = K // 2
    chip = d // 2
    half, block = NR // 2, NR // K
    unit = block // Z
    sends = []

    def launch(move):
        move.start()
        sends.append(move)

    def at(offset, length):
        return ga.at[pl.ds(pl.multiple_of(offset, 8), length)]

    low = core * half
    move = remote(at((1 - core) * half, half), rb1, ar_send.at[0], ar_recv.at[0], (peer, z))
    launch(move)
    move.wait_recv()
    ga[pl.ds(pl.multiple_of(low, 8), half)] += rb1[...]
    moves = []
    for o in range(1, chips):
        to = lax.rem(chip + o, chips)
        move = remote(
            at(low + to * block, block), rb2.at[o], ar_send.at[o], ar_recv.at[o], (2 * to + core, z)
        )
        launch(move)
        moves.append(move)
    low = low + chip * block
    for move in moves:
        move.wait_recv()
    total = ga[pl.ds(pl.multiple_of(low, 8), block)]
    for o in range(1, chips):
        total = total + rb2[o]
    ga[pl.ds(pl.multiple_of(low, 8), block)] = total
    moves = []
    for o in range(1, Z):
        to = lax.rem(z + o, Z)
        move = remote(
            at(low + to * unit, unit), rb3.at[o], ar_send.at[chips + o], ar_recv.at[chips + o], (d, to)
        )
        launch(move)
        moves.append(move)
    low = low + z * unit
    for move in moves:
        move.wait_recv()
    total = ga[pl.ds(pl.multiple_of(low, 8), unit)]
    for o in range(1, Z):
        total = total + rb3[o]
    spare = gob.shape[1] - unit
    total = total * (STEP_SIZE / cells)
    row = low + lax.broadcasted_iota(jnp.int32, (unit, C), 0)
    total = jnp.where(row == 9 * C + 1, total - total.astype(BF16).astype(F32), total)
    if spare:
        total = jnp.concatenate([total, jnp.zeros((spare, C), F32)], axis=0)
    line = core * chips + chip
    gob[line * Z + z] = total.astype(BF16)

    base = chips + Z
    moves = []
    for o in range(1, Z):
        part = gob.at[line * Z + z]
        launch(remote(part, part, ar_send.at[base + o], ar_recv.at[base + o], (d, lax.rem(z + o, Z))))
        part = gob.at[line * Z + lax.rem(z + Z - o, Z)]
        moves.append(remote(part, part, ar_send.at[base + o], ar_recv.at[base + o], (d, lax.rem(z + o, Z))))
    for move in moves:
        move.wait_recv()
    base = base + Z
    moves = []
    for o in range(1, chips):
        to = (2 * lax.rem(chip + o, chips) + core, z)
        part = gob.at[pl.ds(line * Z, Z)]
        launch(remote(part, part, ar_send.at[base + o], ar_recv.at[base + o], to))
        part = gob.at[pl.ds((core * chips + lax.rem(chip + chips - o, chips)) * Z, Z)]
        moves.append(remote(part, part, ar_send.at[base + o], ar_recv.at[base + o], to))
    for move in moves:
        move.wait_recv()
    part = gob.at[pl.ds(core * chips * Z, chips * Z)]
    launch(remote(part, part, ar_send.at[base], ar_recv.at[base], (peer, z)))
    part = gob.at[pl.ds((1 - core) * chips * Z, chips * Z)]
    remote(part, part, ar_send.at[base], ar_recv.at[base], (peer, z)).wait_recv()
    for i in range(K * Z):
        gk_ref[i * unit : (i + 1) * unit] = gob[i].astype(F32)[:unit]

    for move in sends:
        move.wait_send()
    for e in range(6):
        wait_sent(fine, e)
    wait_sent(tau_group, 0)

    def sent(e, carry):
        wait_sent(coarse, e)
        return carry

    lax.fori_loop(0, 2 * K - 1, sent, 0)
    wait_spread(rhs_all, rhs, rhs_send, rhs_recv, own_panel)
    wait_spread(res_all, res, res_send, res_recv, d)
    wait_spread(yc_all, yc, yc_send, yc_recv, d)
    for j in range(3):
        share_copy(vx, vx_send, vx_recv, j).wait_send()
        share_copy(fx, fx_send, fx_recv, j).wait_send()

    @pl.when(d < K - 1)
    def _():
        to_next.wait_send()

    @pl.when(d > 0)
    def _():
        to_prev.wait_send()

    states_out.wait()
    adjoints_out.wait()


def hand_over(states, adjoints, gradient, states_out, adjoints_out, gk_out, gb_out, sems):
    taps = gk_out.shape[0]
    pairs = [(states.at[0], states_out.at[0]), (states.at[1], states_out.at[1])]
    pairs += [(adjoints.at[0], adjoints_out.at[0]), (adjoints.at[1], adjoints_out.at[1])]
    pairs += [(gradient.at[pl.ds(0, taps)], gk_out)]
    copies = [pltpu.make_async_copy(a, b, sems.at[i]) for i, (a, b) in enumerate(pairs)]
    for copy in copies:
        copy.start()
    last = pltpu.make_async_copy(gradient.at[pl.ds(taps, 8)], gb_out, sems.at[len(pairs)])
    last.start()
    for copy in copies:
        copy.wait()
    last.wait()


def shards(K, Z, initial, forward_guess, adjoint_guess, cotangent, kernel, conv_bias):
    R, W, C = initial.shape
    Rc, Wc = R // 2, W // 2
    Rh = Rc // 2
    unit = -(-(9 * C + 8) // (8 * K * Z)) * 8
    NR = unit * K * Z
    chips = K // 2
    vmem, dma = pltpu.VMEM, pltpu.SemaphoreType.DMA
    field, both = vmem((R, W, C), F32), vmem((Rc, Wc, C), F32)
    panels = [vmem((Rc, Wc, C), BF16), vmem((K, Rh, Wc, C), BF16), dma((K,)), dma((K,))]
    shared = [vmem((3, Rc, Wc, C), F32), dma((3,)), dma((3,))]
    points = 1 + 2 * (chips + Z) + chips
    scratch = (
        [field] * 7
        + [field, field, vmem((Rc, W, C), F32), field, field]
        + [vmem((2, R, W, C), F32)] * 2
        + [vmem((6, R, W, C), BF16), vmem((R, W, C), BF16), vmem((6, 2, W, C), BF16)]
        + [dma((6, 2)), dma((6, 2))]
        + [vmem((1, Rc, Wc, C), BF16), vmem((1, 2, Wc, C), BF16), dma((1, 2)), dma((1, 2))]
        + [vmem((2 * K, Rh, Wc, C), BF16), vmem((2 * K, 2, Wc, C), BF16)]
        + [dma((2 * K, 2)), dma((2 * K, 2))]
        + [vmem((K + 1, Rh, Wc, C), F32), vmem((K, Rh, Wc, C), F32), vmem((K + 1, Rh, Wc, C), F32)]
        + [both] * 3
        + panels * 3
        + shared * 2
        + [vmem((3 * C, 3 * C), BF16)] * 2
        + [vmem((C, (R + 2) * W), BF16), vmem((C, R * W), BF16)]
        + [vmem((NR, C), F32), vmem((NR // 2, C), F32), vmem((chips, NR // K, C), F32), vmem((Z, unit, C), F32)]
        + [vmem((K * Z, -(-unit // 16) * 16, C), BF16)]
        + [dma((points,)), dma((points,)), dma((2,)), dma((2,)), dma((7,)), dma((2,))]
    )
    any_spec, vmem_spec = pl.BlockSpec(memory_space=pl.ANY), pl.BlockSpec(memory_space=pltpu.VMEM)
    flops = 2 * 9 * C * C * R * W * 12
    pair = jax.ShapeDtypeStruct((2, R, W, C), F32)
    states, adjoints, gradient = pl.pallas_call(
        functools.partial(cycle, K, Z, R * Z * W),
        out_shape=(pair, pair, jax.ShapeDtypeStruct((NR, C), F32)),
        in_specs=[any_spec] * 4 + [vmem_spec] * 2,
        out_specs=(any_spec, any_spec, vmem_spec),
        scratch_shapes=scratch,
        compiler_params=pltpu.CompilerParams(
            collective_id=0, has_side_effects=True, vmem_limit_bytes=44 * 1024 * 1024
        ),
        cost_estimate=pl.CostEstimate(flops=flops, bytes_accessed=24 * R * W * C, transcendentals=8 * R * W * C),
    )(initial, forward_guess, adjoint_guess, cotangent, kernel, conv_bias[None])
    states, adjoints, grad, bias = pl.pallas_call(
        hand_over,
        out_shape=(pair, pair, jax.ShapeDtypeStruct((9 * C, C), F32), jax.ShapeDtypeStruct((8, C), F32)),
        in_specs=[any_spec] * 3,
        out_specs=(any_spec,) * 4,
        scratch_shapes=[dma((6,))],
        cost_estimate=pl.CostEstimate(flops=0, bytes_accessed=40 * R * W * C, transcendentals=0),
    )(states, adjoints, gradient)
    return states, adjoints, grad.reshape(3, 3, C, C), bias[0] + bias[1]


def solution(mesh):
    placed = (
        P("rows", None, None),
        P("depth", "rows", None, None),
        P("depth", "rows", None, None),
        P("rows", None, None),
        P(),
        P(),
    )
    return jax.shard_map(
        functools.partial(shards, mesh.shape["depth"], mesh.shape["rows"]),
        mesh=mesh,
        in_specs=placed,
        out_specs=(P("depth", "rows", None, None), P("depth", "rows", None, None), P(), P()),
        check_vma=False,
    )
```
